32 devices in a mesh: hid: 8 (over z, x), tok: 4 (over y, core).
Axes of the slice: x: 2, y: 2, z: 4, core: 2. Of those that a mesh axis runs over, the one named last changes fastest.
Arguments:
- tokens: bfloat16 [1024, 12288], P('tok', 'hid'), may hold values from -6 to 6
- cotangent: bfloat16 [1024, 12288], P('tok', 'hid'), may hold values from -0.75 to 0.75
- up_tiles: bfloat16 [4, 1024, 24576], P(None, None, 'hid'), may hold values from -0.09375 to 0.09375
- down_tiles: bfloat16 [4, 24576, 1024], P(None, 'hid'), may hold values from -0.0625 to 0.0625
- block_index: int32 [4, 96, 2], P(None, 'hid'), may hold values from 0 to 2, as said below
- up_left: bfloat16 [12288, 256], P('hid'), may hold values from -0.0546875 to 0.0546875
- up_right: bfloat16 [256, 24576], P(None, 'hid'), may hold values from -0.375 to 0.375
- down_left: bfloat16 [24576, 256], P('hid'), may hold values from -0.0390625 to 0.0390625
- down_right: bfloat16 [256, 12288], P(None, 'hid'), may hold values from -0.375 to 0.375
Outputs:
- layer_out: bfloat16 [1024, 12288], P('tok', 'hid')
- grad_tokens: bfloat16 [1024, 12288], P('tok', 'hid')
- grad_up_tiles: bfloat16 [4, 1024, 24576], P(None, 'tok', 'hid')
- grad_down_tiles: bfloat16 [4, 24576, 1024], P(None, ('hid', 'tok'))
- grad_up_left: bfloat16 [12288, 256], P(('hid', 'tok'))
- grad_up_right: bfloat16 [256, 24576], P('tok', 'hid')
- grad_down_left: bfloat16 [24576, 256], P(('hid', 'tok'))
- grad_down_right: bfloat16 [256, 12288], P('tok', 'hid')
The draws below stay inside these ranges and needn't reach their ends.
Inputs may be any that keep to these rules, and one draw needn't show every extreme that they name: `block_index`: each row names two different sub-blocks.
All inputs are finite; a program needn't handle non-finite values.
Results may differ from the reference program's by a relative error of at most 0.03.
Values may be sent and summed in bfloat16 or wider, within the bound.
A program may use at most 320 MiB of HBM per device.

```python
import jax
import jax.numpy as jnp
from jax import lax

D = 12288
FF = 24576
HB = 256
RANK = 256
TOK_DEV = 256
LEVELS = 4
SUB = 512
NB = 12
FF_BLOCKS = 96
TOKENS = 1024
N_HID = 8
N_TOK = 4


def draw_block_index(key, part):
    first_key = jax.random.fold_in(key, 11)
    second_key = jax.random.fold_in(key, 23)
    excluded = jax.random.randint(first_key, (LEVELS, FF_BLOCKS), 0, 3, dtype=jnp.int32)
    flipped = jax.random.randint(second_key, (LEVELS, FF_BLOCKS), 0, 2, dtype=jnp.int32)
    leading = (excluded + 1 + flipped) % 3
    trailing_axes = (excluded + 2 - flipped) % 3
    return jnp.stack([leading, trailing_axes], axis=-1).astype(jnp.int32)


def block_levels(own_key, dims, shards, low, top_value):
    loudness, own = 1.0, jax.random.fold_in(own_key, 6)
    for dim, parts in shards:
        steps = jnp.exp(jax.random.uniform(jax.random.fold_in(own, dim), (parts,), jnp.float32, low / len(shards), top_value / len(shards)))
        loudness = loudness * jnp.repeat(steps, dims[dim] // parts).reshape([-1 if axis == dim else 1 for axis in range(len(dims))])
    return loudness


def centred(key, extent, scale, limit, pieces=(), kind=jnp.bfloat16):
    drawn = jax.random.normal(key, extent, jnp.float32) * scale
    if len(pieces) > 0:
        drawn = block_levels(key, extent, pieces, -0.22, 0.18) * drawn
    return jnp.clip(drawn, min=-limit, max=limit).astype(kind)


def setup_inputs(seed: int = 0) -> dict:
    arg_keys = jax.random.split(jax.random.key(seed), 10)
    return {
        "tokens": centred(arg_keys[0], (TOKENS, D), 1.0, 6.0, ((0, 4), (1, 8))),
        "cotangent": centred(arg_keys[1], (TOKENS, D), 0.125, 0.75, ((0, 4), (1, 8))),
        "up_tiles": centred(arg_keys[2], (LEVELS, 2 * SUB, FF), (LEVELS * 2 * SUB) ** -0.5, 0.09375, ((2, 8),)),
        "down_tiles": centred(arg_keys[3], (LEVELS, FF, 2 * SUB), (LEVELS * (FF // N_HID) * 2 // 3) ** -0.5, 0.0625, ((1, 8),)),
        "block_index": draw_block_index(jax.random.fold_in(arg_keys[9], 71), 0),
        "up_left": centred(arg_keys[5], (D, RANK), D ** -0.5, 0.0546875, ((0, 8),)),
        "up_right": centred(arg_keys[6], (RANK, FF), RANK ** -0.5, 0.375, ((1, 8),)),
        "down_left": centred(arg_keys[7], (FF, RANK), FF ** -0.5, 0.0390625, ((0, 8),)),
        "down_right": centred(arg_keys[8], (RANK, D), RANK ** -0.5, 0.375, ((1, 8),)),
    }


GELU_SCALE = 0.7978845608028654
GELU_CUBIC = 0.044715


def gelu_parts(pre_act):
    inner = GELU_SCALE * (pre_act + GELU_CUBIC * pre_act * pre_act * pre_act)
    tanh_value = jnp.tanh(inner)
    value = 0.5 * pre_act * (1.0 + tanh_value)
    slope = 0.5 * (1.0 + tanh_value) + 0.5 * pre_act * (1.0 - tanh_value * tanh_value) * GELU_SCALE * (1.0 + 3.0 * GELU_CUBIC * pre_act * pre_act)
    return value, slope


def partner_list(butterfly_level_index):
    devices = jnp.arange(N_HID, dtype=jnp.int32)
    if butterfly_level_index == 0:
        return devices
    return jnp.bitwise_xor(devices, jnp.int32(1 << (butterfly_level_index - 1)))


def round_groups(partials):
    rounded = lax.optimization_barrier(partials.astype(jnp.bfloat16))
    return jnp.sum(rounded.astype(jnp.float32), axis=0).astype(jnp.bfloat16)


def reference(tokens, cotangent, up_tiles, down_tiles, block_index, up_left, up_right, down_left, down_right):
    features = tokens.reshape(TOKENS, N_HID, 3, SUB)
    grad_fields = cotangent.reshape(TOKENS, N_HID, 3, SUB)
    index_all = block_index.reshape(LEVELS, N_HID, NB, 2)
    device_grid = jnp.broadcast_to(jnp.arange(N_HID, dtype=jnp.int32)[:, None, None], (N_HID, NB, 2))
    selectors = (index_all[..., None] == jnp.arange(3, dtype=jnp.int32)).astype(jnp.float32)

    def select_blocks(field, butterfly_level_index):
        moved = field[:, partner_list(butterfly_level_index)]
        return moved[:, device_grid, index_all[butterfly_level_index]]

    def place_blocks(partner_pairs, butterfly_level_index):
        placed_blocks = jnp.einsum("tpbjs,pbjc->tpcs", partner_pairs, selectors[butterfly_level_index], precision=lax.Precision.HIGHEST)
        rounded = placed_blocks.astype(jnp.bfloat16)
        return rounded[:, partner_list(butterfly_level_index)].astype(jnp.float32)

    pre_act = jnp.zeros((TOKENS, N_HID, NB, HB), jnp.float32)
    for partition_key in range(LEVELS):
        chosen = select_blocks(features, partition_key).astype(jnp.float32)
        weights_level = up_tiles[partition_key].reshape(2, SUB, N_HID, NB, HB).astype(jnp.float32)
        pre_act = pre_act + jnp.einsum("tpbjs,jspbh->tpbh", chosen, weights_level)
    low_up = jnp.dot(tokens, up_left, preferred_element_type=jnp.float32).astype(jnp.bfloat16)
    pre_act = pre_act + jnp.dot(low_up, up_right, preferred_element_type=jnp.float32).reshape(TOKENS, N_HID, NB, HB)
    hidden_value, slope = gelu_parts(pre_act)
    hidden_act = hidden_value.astype(jnp.bfloat16)
    hidden_flat = hidden_act.reshape(TOKENS, FF)
    low_down = jnp.dot(hidden_flat, down_left, preferred_element_type=jnp.float32).astype(jnp.bfloat16)
    output_acc = jnp.zeros((TOKENS, N_HID, 3, SUB), jnp.float32)
    for partition_key in range(LEVELS):
        weights_level = down_tiles[partition_key].reshape(N_HID, NB, HB, 2, SUB).astype(jnp.float32)
        partner_pairs = jnp.einsum("tpbh,pbhjs->tpbjs", hidden_act.astype(jnp.float32), weights_level)
        output_acc = output_acc + place_blocks(partner_pairs, partition_key)
    layer_out = (output_acc.reshape(TOKENS, D) + jnp.dot(low_down, down_right, preferred_element_type=jnp.float32)).astype(jnp.bfloat16)

    back_down = jnp.dot(cotangent, down_right.T, preferred_element_type=jnp.float32).astype(jnp.bfloat16)
    grad_hidden = jnp.dot(back_down, down_left.T, preferred_element_type=jnp.float32).reshape(TOKENS, N_HID, NB, HB)
    hidden_groups = hidden_act.astype(jnp.float32).reshape(N_TOK, TOK_DEV, N_HID, NB, HB)
    down_list = []
    for partition_key in range(LEVELS):
        chosen = select_blocks(grad_fields, partition_key).astype(jnp.float32)
        weights_level = down_tiles[partition_key].reshape(N_HID, NB, HB, 2, SUB).astype(jnp.float32)
        grad_hidden = grad_hidden + jnp.einsum("tpbjs,pbhjs->tpbh", chosen, weights_level)
        partials = jnp.einsum("ntpbh,ntpbjs->npbhjs", hidden_groups, chosen.reshape(N_TOK, TOK_DEV, N_HID, NB, 2, SUB))
        down_list.append(round_groups(partials).reshape(FF, 2 * SUB))
    grad_down_tiles = jnp.stack(down_list)
    grad_down_left = round_groups(jnp.einsum("ntf,ntr->nfr", hidden_flat.astype(jnp.float32).reshape(N_TOK, TOK_DEV, FF), back_down.astype(jnp.float32).reshape(N_TOK, TOK_DEV, RANK)))
    grad_down_right = round_groups(jnp.einsum("ntr,ntd->nrd", low_down.astype(jnp.float32).reshape(N_TOK, TOK_DEV, RANK), cotangent.astype(jnp.float32).reshape(N_TOK, TOK_DEV, D)))

    grad_pre = (grad_hidden * slope).astype(jnp.bfloat16)
    grad_flat = grad_pre.reshape(TOKENS, FF)
    back_up = jnp.dot(grad_flat, up_right.T, preferred_element_type=jnp.float32).astype(jnp.bfloat16)
    grad_groups = grad_pre.astype(jnp.float32).reshape(N_TOK, TOK_DEV, N_HID, NB, HB)
    input_acc = jnp.zeros((TOKENS, N_HID, 3, SUB), jnp.float32)
    up_list = []
    for partition_key in range(LEVELS):
        weights_level = up_tiles[partition_key].reshape(2, SUB, N_HID, NB, HB).astype(jnp.float32)
        partner_pairs = jnp.einsum("tpbh,jspbh->tpbjs", grad_pre.astype(jnp.float32), weights_level)
        input_acc = input_acc + place_blocks(partner_pairs, partition_key)
        chosen = select_blocks(features, partition_key).astype(jnp.float32)
        partials = jnp.einsum("ntpbjs,ntpbh->njspbh", chosen.reshape(N_TOK, TOK_DEV, N_HID, NB, 2, SUB), grad_groups)
        up_list.append(round_groups(partials).reshape(2 * SUB, FF))
    grad_up_tiles = jnp.stack(up_list)
    grad_tokens = (input_acc.reshape(TOKENS, D) + jnp.dot(back_up, up_left.T, preferred_element_type=jnp.float32)).astype(jnp.bfloat16)
    grad_up_right = round_groups(jnp.einsum("ntr,ntf->nrf", low_up.astype(jnp.float32).reshape(N_TOK, TOK_DEV, RANK), grad_flat.astype(jnp.float32).reshape(N_TOK, TOK_DEV, FF)))
    grad_up_left = round_groups(jnp.einsum("ntd,ntr->ndr", tokens.astype(jnp.float32).reshape(N_TOK, TOK_DEV, D), back_up.astype(jnp.float32).reshape(N_TOK, TOK_DEV, RANK)))
    return (layer_out, grad_tokens, grad_up_tiles, grad_down_tiles, grad_up_left, grad_up_right, grad_down_left, grad_down_right)
```

```python
import functools
import math

import jax
import jax.numpy as jnp
from jax import lax
from jax.experimental import pallas as pl
from jax.experimental.pallas import tpu as pltpu
from jax.sharding import PartitionSpec as P

GELU_SCALE = 0.7978845608028654
GELU_CUBIC = 0.044715
F32 = jnp.float32
BF16 = jnp.bfloat16
WHOLE = pl.BlockSpec(memory_space=pltpu.VMEM)
VMEM_LIMIT = 56 * 1024 * 1024


def swap(block, axis, mask):
    count = lax.axis_size(axis)
    return lax.ppermute(block, axis, [(i, i ^ mask) for i in range(count)])


def gather_list(block):
    count = lax.axis_size("tok")
    items = {0: block}
    bit = count // 2
    while bit:
        for mask in list(items):
            items[mask | bit] = swap(items[mask], "tok", bit)
        bit //= 2
    return [items[d] for d in range(count)]


def exchange_list(pick):
    me = lax.axis_index("tok")
    return [pick(me)] + [
        swap(pick(me ^ d), "tok", d) for d in range(1, lax.axis_size("tok"))
    ]


def gelu_parts(pre_act):
    inner = GELU_SCALE * (pre_act + GELU_CUBIC * pre_act * pre_act * pre_act)
    tanh_value = jnp.tanh(inner)
    value = 0.5 * pre_act * (1.0 + tanh_value)
    slope = 0.5 * (1.0 + tanh_value) + 0.5 * pre_act * (
        1.0 - tanh_value * tanh_value
    ) * GELU_SCALE * (1.0 + 3.0 * GELU_CUBIC * pre_act * pre_act)
    return (value, slope)


def dot_nn(a, b):
    return jnp.dot(a, b, preferred_element_type=F32)


def dot_nt(a, b):
    return lax.dot_general(a, b, (((1,), (1,)), ((), ())), preferred_element_type=F32)


def split_kernel(levels, parts, sub, *refs):
    feats, (out, own_t) = refs[:levels], refs[levels:]
    width = sub // parts
    for k in range(levels):
        for c in range(3):
            turned = feats[k][:, c * sub : (c + 1) * sub].T
            for p in range(parts):
                out[p, k * 3 + c] = turned[p * width : (p + 1) * width]
            if k == 0:
                own_t[c * sub : (c + 1) * sub, :] = turned


def block_kernel(levels, sub, steps, index, *refs):
    feats, refs = refs[:levels], refs[levels:]
    grads, refs = refs[:levels], refs[levels:]
    low_up, back_down, up, down, up_right, down_left = refs[:6]
    hid_t, grad_pre_out, out_parts, in_parts, low_down, back_up = refs[6:12]
    out_acc, in_acc, low_acc, back_acc = refs[12:]
    b = pl.program_id(0)

    @pl.when(b == 0)
    def _():
        out_acc[...] = jnp.zeros_like(out_acc)
        in_acc[...] = jnp.zeros_like(in_acc)
        low_acc[...] = jnp.zeros_like(low_acc)
        back_acc[...] = jnp.zeros_like(back_acc)

    pre = dot_nn(low_up[...], up_right[...])
    grad = dot_nt(back_down[...], down_left[...])
    pairs = [(k, j) for k in range(levels) for j in range(2)]
    picks = {(k, j): index[(k * steps + b) * 2 + j] for k, j in pairs}
    for k, j in pairs:
        cols = pl.ds(pl.multiple_of(picks[k, j] * sub, sub), sub)
        pre += dot_nn(feats[k][:, cols], up[k, j * sub : (j + 1) * sub, :])
        grad += dot_nt(grads[k][:, cols], down[k, :, j * sub : (j + 1) * sub])
    value, slope = gelu_parts(pre)
    hidden = value.astype(BF16)
    grad_pre = (grad * slope).astype(BF16)
    hid_t[...] = hidden.T
    grad_pre_out[...] = grad_pre
    low_acc[...] += dot_nn(hidden, down_left[...])
    back_acc[...] += dot_nt(grad_pre, up_right[...])
    for k, j in pairs:
        spot = k * 3 + picks[k, j]
        out_acc[spot] += dot_nn(hidden, down[k, :, j * sub : (j + 1) * sub])
        in_acc[spot] += dot_nt(grad_pre, up[k, j * sub : (j + 1) * sub, :])

    @pl.when(b == steps - 1)
    def _():
        for k in range(levels):
            for c in range(3):
                out_parts[k, :, c * sub : (c + 1) * sub] = out_acc[k * 3 + c].astype(BF16)
                in_parts[k, :, c * sub : (c + 1) * sub] = in_acc[k * 3 + c].astype(BF16)
        low_down[...] = low_acc[...].astype(BF16)
        back_up[...] = back_acc[...].astype(BF16)


def down_kernel(levels, sub, groups, blocks, rows, block_width, index, *refs):
    hid, refs = refs[:groups], refs[groups:]
    grads, refs = refs[:groups], refs[groups:]
    backs, (out, out_left) = refs[:groups], refs[groups:]
    i = pl.program_id(0)
    block = (index[levels * blocks * 2] * (pl.num_programs(0) * rows) + i * rows) // block_width
    lhs = [hid[d][...] for d in range(groups)]
    out_left[...] = sum(dot_nn(lhs[d], backs[d][...]) for d in range(groups)).astype(BF16)
    for k in range(levels):
        for j in range(2):
            pick = index[(k * blocks + block) * 2 + j]
            cols = pl.ds(pl.multiple_of(pick * sub, sub), sub)
            total = sum(dot_nn(lhs[d], grads[d][k, :, cols]) for d in range(groups))
            out[k, :, j * sub : (j + 1) * sub] = total.astype(BF16)


def up_kernel(levels, groups, blocks, index, *refs):
    feats, refs = refs[:groups], refs[groups:]
    grads, refs = refs[:groups], refs[groups:]
    lows, (out, out_right) = refs[:groups], refs[groups:]
    b = pl.program_id(0)
    side = index[levels * blocks * 2] // (groups // 2)
    rhs = [grads[d][...] for d in range(groups)]
    out_right[...] = sum(dot_nn(lows[d][...], rhs[d]) for d in range(groups)).astype(BF16)
    for k in range(levels):
        pick = k * 3 + index[(k * blocks + b) * 2 + side]
        total = sum(dot_nn(feats[d][pick], rhs[d]) for d in range(groups))
        out[k] = total.astype(BF16)


def cost(flops, nbytes):
    return pl.CostEstimate(flops=flops, bytes_accessed=nbytes, transcendentals=0)


def on_device(
    tokens, cotangent, up_tiles, down_tiles, block_index, up_left, up_right, down_left, down_right
):
    hid_count = lax.axis_size("hid")
    groups = lax.axis_size("tok")
    me = lax.axis_index("tok")
    levels = hid_count.bit_length()
    rows, feat = tokens.shape
    sub = feat // 3
    blocks = block_index.shape[1]
    hidden = up_tiles.shape[2]
    width = hidden // blocks
    rank = up_left.shape[1]
    parts = groups // 2
    part = sub // parts
    own = hidden // groups
    own_feat = feat // groups
    own_rank = rank // groups
    index = jnp.concatenate([block_index.reshape(-1), me.astype(jnp.int32).reshape(1)])
    params = pltpu.CompilerParams(
        vmem_limit_bytes=VMEM_LIMIT, dimension_semantics=("arbitrary",)
    )
    sds = jax.ShapeDtypeStruct

    lows = lax.psum(
        (dot_nn(tokens, up_left).astype(BF16), dot_nt(cotangent, down_right).astype(BF16)), "hid"
    )
    low_up, back_down = lows
    feats = [tokens] + [swap(tokens, "hid", 1 << k) for k in range(levels - 1)]
    grads = [cotangent] + [swap(cotangent, "hid", 1 << k) for k in range(levels - 1)]

    split, own_t = pl.pallas_call(
        functools.partial(split_kernel, levels, parts, sub),
        out_shape=(sds((parts, levels * 3, part, rows), BF16), sds((feat, rows), BF16)),
        in_specs=[WHOLE] * levels,
        out_specs=(WHOLE, WHOLE),
        compiler_params=pltpu.CompilerParams(vmem_limit_bytes=VMEM_LIMIT),
        cost_estimate=cost(0, 4 * levels * rows * feat),
    )(*feats)
    feat_items = exchange_list(
        lambda q: lax.dynamic_index_in_dim(split, q % parts, 0, keepdims=False)
    )
    own_items = exchange_list(
        lambda q: lax.dynamic_slice_in_dim(own_t, q * own_feat, own_feat, 0)
    )
    grad_items = gather_list(jnp.stack(grads))
    low_up_items = exchange_list(
        lambda q: lax.dynamic_slice_in_dim(low_up.T, q * own_rank, own_rank, 0)
    )
    back_down_items = gather_list(back_down)

    per_set = 2 * rows * hidden * levels * 2 * sub
    whole3 = lambda i, idx: (0, 0, 0)
    whole2 = lambda i, idx: (0, 0)
    hid_t, grad_pre, out_parts, in_parts, low_down, back_up = pl.pallas_call(
        functools.partial(block_kernel, levels, sub, blocks),
        grid_spec=pltpu.PrefetchScalarGridSpec(
            num_scalar_prefetch=1,
            grid=(blocks,),
            in_specs=[WHOLE] * (2 * levels + 2)
            + [
                pl.BlockSpec((levels, 2 * sub, width), lambda i, idx: (0, 0, i)),
                pl.BlockSpec((levels, width, 2 * sub), lambda i, idx: (0, i, 0)),
                pl.BlockSpec((rank, width), lambda i, idx: (0, i)),
                pl.BlockSpec((width, rank), lambda i, idx: (i, 0)),
            ],
            out_specs=[
                pl.BlockSpec((width, rows), lambda i, idx: (i, 0)),
                pl.BlockSpec((rows, width), lambda i, idx: (0, i)),
                pl.BlockSpec((levels, rows, feat), whole3),
                pl.BlockSpec((levels, rows, feat), whole3),
                pl.BlockSpec((rows, rank), whole2),
                pl.BlockSpec((rows, rank), whole2),
            ],
            scratch_shapes=[
                pltpu.VMEM((levels * 3, rows, sub), F32),
                pltpu.VMEM((levels * 3, rows, sub), F32),
                pltpu.VMEM((rows, rank), F32),
                pltpu.VMEM((rows, rank), F32),
            ],
        ),
        out_shape=(
            sds((hidden, rows), BF16),
            sds((rows, hidden), BF16),
            sds((levels, rows, feat), BF16),
            sds((levels, rows, feat), BF16),
            sds((rows, rank), BF16),
            sds((rows, rank), BF16),
        ),
        compiler_params=params,
        cost_estimate=cost(4 * per_set, 4 * levels * hidden * 2 * sub),
    )(index, *feats, *grads, low_up, back_down, up_tiles, down_tiles, up_right, down_left)

    low_down, back_up = lax.psum((low_down, back_up), "hid")
    grad_pre_items = gather_list(grad_pre)
    hid_items = exchange_list(lambda q: lax.dynamic_slice_in_dim(hid_t, q * own, own, 0))
    out_got = [swap(out_parts[k], "hid", 1 << (k - 1)) for k in range(1, levels)]
    in_got = [swap(in_parts[k], "hid", 1 << (k - 1)) for k in range(1, levels)]

    chunk = math.gcd(own, width)
    grad_down_tiles, grad_down_left = pl.pallas_call(
        functools.partial(down_kernel, levels, sub, groups, blocks, chunk, width),
        grid_spec=pltpu.PrefetchScalarGridSpec(
            num_scalar_prefetch=1,
            grid=(own // chunk,),
            in_specs=[pl.BlockSpec((chunk, rows), lambda i, idx: (i, 0))] * groups
            + [WHOLE] * (2 * groups),
            out_specs=[
                pl.BlockSpec((levels, chunk, 2 * sub), lambda i, idx: (0, i, 0)),
                pl.BlockSpec((chunk, rank), lambda i, idx: (i, 0)),
            ],
        ),
        out_shape=(sds((levels, own, 2 * sub), BF16), sds((own, rank), BF16)),
        compiler_params=params,
        cost_estimate=cost(per_set, 2 * levels * (rows * groups * feat + own * 2 * sub)),
    )(index, *hid_items, *grad_items, *back_down_items)

    grad_up_tiles, grad_up_right = pl.pallas_call(
        functools.partial(up_kernel, levels, groups, blocks),
        grid_spec=pltpu.PrefetchScalarGridSpec(
            num_scalar_prefetch=1,
            grid=(blocks,),
            in_specs=[WHOLE] * groups
            + [pl.BlockSpec((rows, width), lambda i, idx: (0, i))] * groups
            + [WHOLE] * groups,
            out_specs=[
                pl.BlockSpec((levels, part, width), lambda i, idx: (0, 0, i)),
                pl.BlockSpec((own_rank, width), lambda i, idx: (0, i)),
            ],
        ),
        out_shape=(sds((levels, part, hidden), BF16), sds((own_rank, hidden), BF16)),
        compiler_params=params,
        cost_estimate=cost(per_set, 2 * levels * part * hidden + 4 * rows * groups * hidden),
    )(index, *feat_items, *grad_pre_items, *low_up_items)

    low_down_items = exchange_list(
        lambda q: lax.dynamic_slice_in_dim(low_down.T, q * own_rank, own_rank, 0)
    )
    back_up_items = gather_list(back_up)
    grad_down_right = sum(
        dot_nn(low_down_items[d], grad_items[d][0]) for d in range(groups)
    ).astype(BF16)
    grad_up_left = sum(
        dot_nn(own_items[d], back_up_items[d]) for d in range(groups)
    ).astype(BF16)

    def finish(own_part, got, left, right_dot):
        total = own_part.astype(F32)
        for item in got:
            total = total + item.astype(F32)
        return (total + right_dot(left)).astype(BF16)

    layer_out = finish(out_parts[0], out_got, low_down, lambda v: dot_nn(v, down_right))
    grad_tokens = finish(in_parts[0], in_got, back_up, lambda v: dot_nt(v, up_left))
    return (
        layer_out,
        grad_tokens,
        grad_up_tiles,
        grad_down_tiles,
        grad_up_left,
        grad_up_right,
        grad_down_left,
        grad_down_right,
    )


def solution(mesh):
    return jax.shard_map(
        on_device,
        mesh=mesh,
        in_specs=(
            P("tok", "hid"),
            P("tok", "hid"),
            P(None, None, "hid"),
            P(None, "hid", None),
            P(None, "hid", None),
            P("hid", None),
            P(None, "hid"),
            P("hid", None),
            P(None, "hid"),
        ),
        out_specs=(
            P("tok", "hid"),
            P("tok", "hid"),
            P(None, "tok", "hid"),
            P(None, ("hid", "tok"), None),
            P(("hid", "tok"), None),
            P("tok", "hid"),
            P(("hid", "tok"), None),
            P("tok", "hid"),
        ),
        check_vma=False,
    )
```

```python
import functools
import math

import jax
import jax.numpy as jnp
from jax import lax
from jax.experimental import pallas as pl
from jax.experimental.pallas import tpu as pltpu
from jax.sharding import PartitionSpec as P

GELU_SCALE = 0.7978845608028654
GELU_CUBIC = 0.044715
F32 = jnp.float32
BF16 = jnp.bfloat16
WHOLE = pl.BlockSpec(memory_space=pltpu.VMEM)
VMEM_LIMIT = 56 * 1024 * 1024


def swap(block, axis, mask):
    count = lax.axis_size(axis)
    return lax.ppermute(block, axis, [(i, i ^ mask) for i in range(count)])


def gather_list(block):
    count = lax.axis_size("tok")
    items = {0: block}
    bit = count // 2
    while bit:
        for mask in list(items):
            items[mask | bit] = swap(items[mask], "tok", bit)
        bit //= 2
    return [items[d] for d in range(count)]


def exchange_list(pick):
    me = lax.axis_index("tok")
    return [pick(me)] + [
        swap(pick(me ^ d), "tok", d) for d in range(1, lax.axis_size("tok"))
    ]


def sum_hid(block):
    mask = 1
    while mask < lax.axis_size("hid"):
        block = (block.astype(F32) + swap(block, "hid", mask).astype(F32)).astype(BF16)
        mask *= 2
    return block


def gelu_parts(pre_act):
    inner = GELU_SCALE * (pre_act + GELU_CUBIC * pre_act * pre_act * pre_act)
    tanh_value = jnp.tanh(inner)
    value = 0.5 * pre_act * (1.0 + tanh_value)
    slope = 0.5 * (1.0 + tanh_value) + 0.5 * pre_act * (
        1.0 - tanh_value * tanh_value
    ) * GELU_SCALE * (1.0 + 3.0 * GELU_CUBIC * pre_act * pre_act)
    return (value, slope)


def dot_nn(a, b):
    return jnp.dot(a, b, preferred_element_type=F32)


def dot_nt(a, b):
    return lax.dot_general(a, b, (((1,), (1,)), ((), ())), preferred_element_type=F32)


def split_kernel(levels, parts, sub, *refs):
    feats, (out, own_t) = refs[:levels], refs[levels:]
    width = sub // parts
    for k in range(levels):
        for c in range(3):
            turned = feats[k][:, c * sub : (c + 1) * sub].T
            for p in range(parts):
                out[p, k * 3 + c] = turned[p * width : (p + 1) * width]
            if k == 0:
                own_t[c * sub : (c + 1) * sub, :] = turned


def block_kernel(levels, sub, steps, index, *refs):
    feats, refs = refs[:levels], refs[levels:]
    grads, refs = refs[:levels], refs[levels:]
    low_up, back_down, up, down, up_right, down_left = refs[:6]
    hid_t, grad_pre_out, out_parts, in_parts, low_down, back_up = refs[6:12]
    out_acc, in_acc, low_acc, back_acc = refs[12:]
    b = pl.program_id(0)

    @pl.when(b == 0)
    def _():
        out_acc[...] = jnp.zeros_like(out_acc)
        in_acc[...] = jnp.zeros_like(in_acc)
        low_acc[...] = jnp.zeros_like(low_acc)
        back_acc[...] = jnp.zeros_like(back_acc)

    pre = dot_nn(low_up[...], up_right[...])
    grad = dot_nt(back_down[...], down_left[...])
    pairs = [(k, j) for k in range(levels) for j in range(2)]
    picks = {(k, j): index[(k * steps + b) * 2 + j] for k, j in pairs}
    for k, j in pairs:
        cols = pl.ds(pl.multiple_of(picks[k, j] * sub, sub), sub)
        pre += dot_nn(feats[k][:, cols], up[k, j * sub : (j + 1) * sub, :])
        grad += dot_nt(grads[k][:, cols], down[k, :, j * sub : (j + 1) * sub])
    value, slope = gelu_parts(pre)
    hidden = value.astype(BF16)
    grad_pre = (grad * slope).astype(BF16)
    hid_t[...] = hidden.T
    grad_pre_out[...] = grad_pre
    low_acc[...] += dot_nn(hidden, down_left[...])
    back_acc[...] += dot_nt(grad_pre, up_right[...])
    for k, j in pairs:
        spot = k * 3 + picks[k, j]
        out_acc[spot] += dot_nn(hidden, down[k, :, j * sub : (j + 1) * sub])
        in_acc[spot] += dot_nt(grad_pre, up[k, j * sub : (j + 1) * sub, :])

    @pl.when(b == steps - 1)
    def _():
        for k in range(levels):
            for c in range(3):
                out_parts[k, :, c * sub : (c + 1) * sub] = out_acc[k * 3 + c].astype(BF16)
                in_parts[k, :, c * sub : (c + 1) * sub] = in_acc[k * 3 + c].astype(BF16)
        low_down[...] = low_acc[...].astype(BF16)
        back_up[...] = back_acc[...].astype(BF16)


def down_kernel(levels, sub, groups, blocks, rows, block_width, index, *refs):
    hid, refs = refs[:groups], refs[groups:]
    grads, refs = refs[:groups], refs[groups:]
    backs, (out, out_left) = refs[:groups], refs[groups:]
    i = pl.program_id(0)
    block = (index[levels * blocks * 2] * (pl.num_programs(0) * rows) + i * rows) // block_width
    lhs = [hid[d][...] for d in range(groups)]
    out_left[...] = sum(dot_nn(lhs[d], backs[d][...]) for d in range(groups)).astype(BF16)
    for k in range(levels):
        for j in range(2):
            pick = index[(k * blocks + block) * 2 + j]
            cols = pl.ds(pl.multiple_of(pick * sub, sub), sub)
            total = sum(dot_nn(lhs[d], grads[d][k, :, cols]) for d in range(groups))
            out[k, :, j * sub : (j + 1) * sub] = total.astype(BF16)


def up_kernel(levels, groups, blocks, index, *refs):
    feats, refs = refs[:groups], refs[groups:]
    grads, refs = refs[:groups], refs[groups:]
    lows, (out, out_right) = refs[:groups], refs[groups:]
    b = pl.program_id(0)
    side = index[levels * blocks * 2] // (groups // 2)
    rhs = [grads[d][...] for d in range(groups)]
    out_right[...] = sum(dot_nn(lows[d][...], rhs[d]) for d in range(groups)).astype(BF16)
    for k in range(levels):
        pick = k * 3 + index[(k * blocks + b) * 2 + side]
        total = sum(dot_nn(feats[d][pick], rhs[d]) for d in range(groups))
        out[k] = total.astype(BF16)


def cost(flops, nbytes):
    return pl.CostEstimate(flops=flops, bytes_accessed=nbytes, transcendentals=0)


def on_device(
    tokens, cotangent, up_tiles, down_tiles, block_index, up_left, up_right, down_left, down_right
):
    hid_count = lax.axis_size("hid")
    groups = lax.axis_size("tok")
    me = lax.axis_index("tok")
    levels = hid_count.bit_length()
    rows, feat = tokens.shape
    sub = feat // 3
    blocks = block_index.shape[1]
    hidden = up_tiles.shape[2]
    width = hidden // blocks
    rank = up_left.shape[1]
    parts = groups // 2
    part = sub // parts
    own = hidden // groups
    own_feat = feat // groups
    own_rank = rank // groups
    index = jnp.concatenate([block_index.reshape(-1), me.astype(jnp.int32).reshape(1)])
    params = pltpu.CompilerParams(
        vmem_limit_bytes=VMEM_LIMIT, dimension_semantics=("arbitrary",)
    )
    sds = jax.ShapeDtypeStruct

    lows = sum_hid(
        jnp.stack(
            [dot_nn(tokens, up_left).astype(BF16), dot_nt(cotangent, down_right).astype(BF16)]
        )
    )
    low_up, back_down = lows
    feats = [tokens] + [swap(tokens, "hid", 1 << k) for k in range(levels - 1)]
    grads = [cotangent] + [swap(cotangent, "hid", 1 << k) for k in range(levels - 1)]

    split, own_t = pl.pallas_call(
        functools.partial(split_kernel, levels, parts, sub),
        out_shape=(sds((parts, levels * 3, part, rows), BF16), sds((feat, rows), BF16)),
        in_specs=[WHOLE] * levels,
        out_specs=(WHOLE, WHOLE),
        compiler_params=pltpu.CompilerParams(vmem_limit_bytes=VMEM_LIMIT),
        cost_estimate=cost(0, 4 * levels * rows * feat),
    )(*feats)
    feat_items = exchange_list(
        lambda q: lax.dynamic_index_in_dim(split, q % parts, 0, keepdims=False)
    )
    own_items = exchange_list(
        lambda q: lax.dynamic_slice_in_dim(own_t, q * own_feat, own_feat, 0)
    )
    grad_items = gather_list(jnp.stack(grads))
    low_up_items = exchange_list(
        lambda q: lax.dynamic_slice_in_dim(low_up.T, q * own_rank, own_rank, 0)
    )
    back_down_items = gather_list(back_down)

    per_set = 2 * rows * hidden * levels * 2 * sub
    whole3 = lambda i, idx: (0, 0, 0)
    whole2 = lambda i, idx: (0, 0)
    hid_t, grad_pre, out_parts, in_parts, low_down, back_up = pl.pallas_call(
        functools.partial(block_kernel, levels, sub, blocks),
        grid_spec=pltpu.PrefetchScalarGridSpec(
            num_scalar_prefetch=1,
            grid=(blocks,),
            in_specs=[WHOLE] * (2 * levels + 2)
            + [
                pl.BlockSpec((levels, 2 * sub, width), lambda i, idx: (0, 0, i)),
                pl.BlockSpec((levels, width, 2 * sub), lambda i, idx: (0, i, 0)),
                pl.BlockSpec((rank, width), lambda i, idx: (0, i)),
                pl.BlockSpec((width, rank), lambda i, idx: (i, 0)),
            ],
            out_specs=[
                pl.BlockSpec((width, rows), lambda i, idx: (i, 0)),
                pl.BlockSpec((rows, width), lambda i, idx: (0, i)),
                pl.BlockSpec((levels, rows, feat), whole3),
                pl.BlockSpec((levels, rows, feat), whole3),
                pl.BlockSpec((rows, rank), whole2),
                pl.BlockSpec((rows, rank), whole2),
            ],
            scratch_shapes=[
                pltpu.VMEM((levels * 3, rows, sub), F32),
                pltpu.VMEM((levels * 3, rows, sub), F32),
                pltpu.VMEM((rows, rank), F32),
                pltpu.VMEM((rows, rank), F32),
            ],
        ),
        out_shape=(
            sds((hidden, rows), BF16),
            sds((rows, hidden), BF16),
            sds((levels, rows, feat), BF16),
            sds((levels, rows, feat), BF16),
            sds((rows, rank), BF16),
            sds((rows, rank), BF16),
        ),
        compiler_params=params,
        cost_estimate=cost(4 * per_set, 4 * levels * hidden * 2 * sub),
    )(index, *feats, *grads, low_up, back_down, up_tiles, down_tiles, up_right, down_left)

    low_down, back_up = sum_hid(jnp.stack([low_down, back_up]))
    grad_pre_items = gather_list(grad_pre)
    hid_items = exchange_list(lambda q: lax.dynamic_slice_in_dim(hid_t, q * own, own, 0))
    out_got = [swap(out_parts[k], "hid", 1 << (k - 1)) for k in range(1, levels)]
    in_got = [swap(in_parts[k], "hid", 1 << (k - 1)) for k in range(1, levels)]

    chunk = math.gcd(own, width)
    grad_down_tiles, grad_down_left = pl.pallas_call(
        functools.partial(down_kernel, levels, sub, groups, blocks, chunk, width),
        grid_spec=pltpu.PrefetchScalarGridSpec(
            num_scalar_prefetch=1,
            grid=(own // chunk,),
            in_specs=[pl.BlockSpec((chunk, rows), lambda i, idx: (i, 0))] * groups
            + [WHOLE] * (2 * groups),
            out_specs=[
                pl.BlockSpec((levels, chunk, 2 * sub), lambda i, idx: (0, i, 0)),
                pl.BlockSpec((chunk, rank), lambda i, idx: (i, 0)),
            ],
        ),
        out_shape=(sds((levels, own, 2 * sub), BF16), sds((own, rank), BF16)),
        compiler_params=params,
        cost_estimate=cost(per_set, 2 * levels * (rows * groups * feat + own * 2 * sub)),
    )(index, *hid_items, *grad_items, *back_down_items)

    grad_up_tiles, grad_up_right = pl.pallas_call(
        functools.partial(up_kernel, levels, groups, blocks),
        grid_spec=pltpu.PrefetchScalarGridSpec(
            num_scalar_prefetch=1,
            grid=(blocks,),
            in_specs=[WHOLE] * groups
            + [pl.BlockSpec((rows, width), lambda i, idx: (0, i))] * groups
            + [WHOLE] * groups,
            out_specs=[
                pl.BlockSpec((levels, part, width), lambda i, idx: (0, 0, i)),
                pl.BlockSpec((own_rank, width), lambda i, idx: (0, i)),
            ],
        ),
        out_shape=(sds((levels, part, hidden), BF16), sds((own_rank, hidden), BF16)),
        compiler_params=params,
        cost_estimate=cost(per_set, 2 * levels * part * hidden + 4 * rows * groups * hidden),
    )(index, *feat_items, *grad_pre_items, *low_up_items)

    low_down_items = exchange_list(
        lambda q: lax.dynamic_slice_in_dim(low_down.T, q * own_rank, own_rank, 0)
    )
    back_up_items = gather_list(back_up)
    grad_down_right = sum(
        dot_nn(low_down_items[d], grad_items[d][0]) for d in range(groups)
    ).astype(BF16)
    grad_up_left = sum(
        dot_nn(own_items[d], back_up_items[d]) for d in range(groups)
    ).astype(BF16)

    def finish(own_part, got, left, right_dot):
        total = own_part.astype(F32)
        for item in got:
            total = total + item.astype(F32)
        return (total + right_dot(left)).astype(BF16)

    layer_out = finish(out_parts[0], out_got, low_down, lambda v: dot_nn(v, down_right))
    grad_tokens = finish(in_parts[0], in_got, back_up, lambda v: dot_nt(v, up_left))
    return (
        layer_out,
        grad_tokens,
        grad_up_tiles,
        grad_down_tiles,
        grad_up_left,
        grad_up_right,
        grad_down_left,
        grad_down_right,
    )


def solution(mesh):
    return jax.shard_map(
        on_device,
        mesh=mesh,
        in_specs=(
            P("tok", "hid"),
            P("tok", "hid"),
            P(None, None, "hid"),
            P(None, "hid", None),
            P(None, "hid", None),
            P("hid", None),
            P(None, "hid"),
            P("hid", None),
            P(None, "hid"),
        ),
        out_specs=(
            P("tok", "hid"),
            P("tok", "hid"),
            P(None, "tok", "hid"),
            P(None, ("hid", "tok"), None),
            P(("hid", "tok"), None),
            P("tok", "hid"),
            P(("hid", "tok"), None),
            P("tok", "hid"),
        ),
        check_vma=False,
    )
```
